32 devices in a mesh: row: 4 (over y, x), col: 8 (over z, core).
Axes of the slice: x: 2, y: 2, z: 4, core: 2. Of those that a mesh axis runs over, the one named last changes fastest.
Arguments:
- base_input: bfloat16 [1024, 16384], P('col', 'row'), may hold values from -6 to 6
- layer_input: bfloat16 [1024, 16384], P('row', 'col'), may hold values from -6 to 6
- out_grad: bfloat16 [1024, 16384], P('col', 'row'), may hold values from -6 to 6
- cross_weight: bfloat16 [16384, 16384], P('row', 'col'), may hold values from -0.046875 to 0.046875
- cross_bias: bfloat16 [16384], P('row'), may hold values from -5 to 5
Outputs:
- weight_grad: float32 [16384, 16384], P('row', 'col')
- bias_grad: float32 [16384], P('row')
- base_grad: bfloat16 [1024, 16384], P('col', 'row')
- branch_grad: bfloat16 [1024, 16384], P('row', 'col')
The draws below stay inside these ranges and needn't reach their ends.
All inputs are finite; a program needn't handle non-finite values.
Results may differ from the reference program's by a relative error of at most 0.019.
Values may be sent and summed in bfloat16 or wider, within the bound.
No kernel may reach another device: no remote copies, remote signals or barrier semaphores. Data moves between devices by JAX's collectives and lax.ppermute only.
A program may use at most 128 MiB of HBM per device.

```python
import jax
import jax.numpy as jnp
from jax import lax

D = 16384
EXAMPLES = 1024
N_ROW = 4
N_COL = 8


def steps_of(key, dims, shards, smallest, largest):
    level, own = 1.0, jax.random.fold_in(key, 6)
    for axis_at, shards_of in shards:
        steps = jnp.exp(jax.random.uniform(jax.random.fold_in(own, axis_at), (shards_of,), jnp.float32, smallest / len(shards), largest / len(shards)))
        level = level * jnp.repeat(steps, dims[axis_at] // shards_of).reshape([-1 if axis == axis_at else 1 for axis in range(len(dims))])
    return level


def centred(own_key, shape, deviation, reach, shards=(), held_as=jnp.bfloat16):
    entries = jax.random.normal(own_key, shape, jnp.float32) * deviation
    if len(shards) > 0:
        entries = steps_of(own_key, shape, shards, -0.22, 0.18) * entries
    return jnp.clip(entries, min=-reach, max=reach).astype(held_as)


def setup_inputs(seed: int = 0) -> dict:
    arg_keys = jax.random.split(jax.random.key(seed), 6)
    base_input = centred(arg_keys[0], (EXAMPLES, D), 1.0, 6.0, ((0, 8), (1, 4)))
    layer_input = centred(arg_keys[1], (EXAMPLES, D), 1.0, 6.0, ((0, 4), (1, 8)))
    out_grad = centred(arg_keys[2], (EXAMPLES, D), 1.0, 6.0, ((0, 8), (1, 4)))
    cross_weight = centred(arg_keys[3], (D, D), D ** -0.5, 0.046875, ((0, 4), (1, 8)))
    cross_bias = centred(arg_keys[4], (D,), 1.0, 5.0, ((0, 4),))
    return {"base_input": base_input, "layer_input": layer_input, "out_grad": out_grad, "cross_weight": cross_weight, "cross_bias": cross_bias}


def reference(base_input, layer_input, out_grad, cross_weight, cross_bias):
    hidden_grad = (out_grad.astype(jnp.float32) * base_input.astype(jnp.float32)).astype(jnp.bfloat16)
    weight_grad = jnp.dot(hidden_grad.T, layer_input, preferred_element_type=jnp.float32)
    bias_grad = jnp.sum(hidden_grad.astype(jnp.float32), axis=0)
    in_block = D // N_COL
    out_block = D // N_ROW

    def pre_step(total, index):
        start = (index * in_block).astype(jnp.int32)
        rows = lax.dynamic_slice_in_dim(layer_input, start, in_block, 1)
        cols = lax.dynamic_slice_in_dim(cross_weight, start, in_block, 1)
        part = jnp.dot(rows, cols.T, preferred_element_type=jnp.float32).astype(jnp.bfloat16)
        return total + part.astype(jnp.float32), None

    zeros = jnp.zeros((EXAMPLES, D), jnp.float32)
    preact, _ = lax.scan(pre_step, zeros, jnp.arange(N_COL, dtype=jnp.int32))
    preact = preact + cross_bias.astype(jnp.float32)[None, :]
    base_grad = (out_grad.astype(jnp.float32) * preact).astype(jnp.bfloat16)

    def back_step(total, index):
        start = (index * out_block).astype(jnp.int32)
        rows = lax.dynamic_slice_in_dim(hidden_grad, start, out_block, 1)
        block = lax.dynamic_slice_in_dim(cross_weight, start, out_block, 0)
        part = jnp.dot(rows, block, preferred_element_type=jnp.float32).astype(jnp.bfloat16)
        return total + part.astype(jnp.float32), None

    branch, _ = lax.scan(back_step, zeros, jnp.arange(N_ROW, dtype=jnp.int32))
    branch_grad = branch.astype(jnp.bfloat16)
    return (weight_grad, bias_grad, base_grad, branch_grad)
```

```python
import functools

import jax
import jax.numpy as jnp
from jax import lax
from jax.experimental import pallas as pl
from jax.experimental.pallas import tpu as pltpu
from jax.sharding import PartitionSpec as P

F32, BF16 = jnp.float32, jnp.bfloat16
ANY = pl.BlockSpec(memory_space=pl.ANY)
SMEM = pl.BlockSpec(memory_space=pltpu.SMEM)
VMEM = pl.BlockSpec(memory_space=pltpu.VMEM)
DMA = pltpu.SemaphoreType.DMA
MIB = 1024 * 1024

CORE, Z, ROW, FIRST, REL = range(5)
PIECES = 2


def params(mib):
    return pltpu.CompilerParams(vmem_limit_bytes=mib * MIB)


def in_hbm(*arrays):
    return [pltpu.with_memory_space_constraint(a, pltpu.HBM) for a in arrays]


def cost(flops, nbytes):
    return pl.CostEstimate(flops=1, bytes_accessed=1, transcendentals=0)


def turned(place, apart):
    other = jnp.where(apart == 1, 2, jnp.where(apart == 2, 1, apart))
    return jnp.where(place[CORE] == 0, apart, other)


def x_sources(place, block, half, own, got):
    lanes = own.shape[0] // 2
    apart = turned(place, block ^ place[ROW])
    last = place[REL] == 3
    conds = [apart == 0, apart == 1]
    conds.append(jnp.where(last, apart == 3, apart == 2))
    conds.append(jnp.where(last, apart == 2, apart == 3))
    refs = (own,) + tuple(got)
    return [(ref.at[pl.ds(half * lanes, lanes)], cond) for ref, cond in zip(refs, conds) if ref is not None]


def load_x(place, block, own, got, held, at, sem):
    for half in range(2):
        slot = at + jnp.where(place[CORE] == half, 0, 1)
        for ref, cond in x_sources(place, block, half, own, got):

            @pl.when(cond)
            def _():
                pltpu.make_async_copy(ref, held.at[slot], sem.at[slot]).start()


def wait_x(own, held, at, sem):
    lanes = own.shape[0] // 2
    for k in (at, at + 1):
        pltpu.make_async_copy(own.at[pl.ds(0, lanes)], held.at[k], sem.at[k]).wait()


def pre_block(place, index):
    middle = jnp.logical_or(place[Z] == 1, place[Z] == 2)
    rel = {0: 0, 1: 1, 2: jnp.where(middle, 3, 2), 3: jnp.where(middle, 2, 3)}[index]
    return rel ^ place[FIRST]


def back_block(place, slot):
    low = place[Z] < 2
    return (place[Z], place[Z] ^ 1, jnp.where(low, 2, 1), jnp.where(low, 3, 0))[slot]


def pre_kernel(indices, n_got, chunks, place, own, *refs):
    got = list(refs[:n_got]) + [None] * (3 - n_got)
    w, refs = refs[n_got], refs[n_got + 1 :]
    n_out = 2 * len(indices)
    n_ref = (1 + PIECES) * len(indices)
    outs, (held, held_w, held_y, sem, sem_w, sem_y) = refs[:n_ref], refs[n_ref:]
    lanes = held.shape[1]
    tile = w.shape[0] // chunks

    def w_copy(i):
        part = pl.ds(pl.multiple_of(i * tile, tile), tile)
        return pltpu.make_async_copy(w.at[part], held_w.at[part], sem_w.at[i])

    def y_copy(i, k, out, at):
        part = pl.ds(pl.multiple_of(at * tile, tile), tile)
        return pltpu.make_async_copy(held_y.at[i, pl.ds(k * lanes, lanes)], out.at[:, part], sem_y.at[i, k])

    def start_y(i):
        run = chunks // PIECES
        for b in range(len(indices)):
            mine, *other = outs[(1 + PIECES) * b : (1 + PIECES) * (b + 1)]
            y_copy(i, 2 * b, mine, i).start()
            for piece, out in enumerate(other):

                @pl.when(i // run == piece)
                def _():
                    y_copy(i, 2 * b + 1, out, i % run).start()

    for i, index in enumerate(indices):
        load_x(place, pre_block(place, index), own, got, held, 2 * i, sem)

    def start(i, _):
        w_copy(i).start()
        return _

    lax.fori_loop(0, chunks, start, 0)
    for i in range(len(indices)):
        wait_x(own, held, 2 * i, sem)

    def step(i, _):
        w_copy(i).wait()
        x = held[...].reshape(n_out * lanes, held.shape[2])
        rows = held_w[pl.ds(pl.multiple_of(i * tile, tile), tile)]
        held_y[i] = lax.dot_general(x, rows, (((1,), (1,)), ((), ())), preferred_element_type=F32).astype(BF16)
        start_y(i)
        return _

    lax.fori_loop(0, chunks, step, 0)

    def finish(i, _):
        for k in range(n_out):
            y_copy(i, k, outs[0], 0).wait()
        return _

    lax.fori_loop(0, chunks, finish, 0)


def pre_parts(place, own, got, w, indices, chunks):
    rows, depth = own.shape
    lanes, wide, outs = rows // 2, w.shape[0], 2 * len(indices)
    return pl.pallas_call(
        functools.partial(pre_kernel, tuple(indices), len(got), chunks),
        in_specs=[SMEM] + [ANY] * (2 + len(got)),
        out_specs=[ANY] * ((1 + PIECES) * len(indices)),
        scratch_shapes=[
            pltpu.VMEM((outs, lanes, depth), BF16),
            pltpu.VMEM((wide, depth), BF16),
            pltpu.VMEM((chunks, outs * lanes, wide // chunks), BF16),
            DMA((outs,)),
            DMA((chunks,)),
            DMA((chunks, outs)),
        ],
        out_shape=[jax.ShapeDtypeStruct((lanes, n), BF16) for n in [wide] + [wide // PIECES] * PIECES]
        * len(indices),
        compiler_params=params(28),
        cost_estimate=cost(2 * outs * lanes * depth * wide, 2 * wide * depth),
        name="pre_parts",
    )(place, *in_hbm(own, *got, w))


def back_kernel(slots, by_role, n_prior, chunks, place, *refs):
    n_h = 2 * len(slots)
    hs, w, refs = refs[:n_h], refs[n_h], refs[n_h + 1 + n_prior :]
    outs, (held, held_w, held_y, sem, sem_w, sem_y) = refs[:-6], refs[-6:]
    lanes = held.shape[1]
    tile = w.shape[1] // chunks

    def w_copy(i):
        part = pl.ds(pl.multiple_of(i * tile, tile), tile)
        return pltpu.make_async_copy(w.at[:, part], held_w.at[i], sem_w.at[i])

    def h_copy(k):
        slot = k // 2 * 2 + (place[CORE] if k % 2 == 0 else 1 - place[CORE])
        return pltpu.make_async_copy(hs[k], held.at[slot], sem.at[k])

    def y_copy(i, k, out):
        part = pl.ds(pl.multiple_of(i * tile, tile), tile)
        return pltpu.make_async_copy(held_y.at[i, pl.ds(2 * k * lanes, 2 * lanes)], out.at[:, part], sem_y.at[i, k])

    def start_y(i, k):
        if not by_role:
            y_copy(i, k, outs[k]).start()
            return
        role = turned(place, back_block(place, slots[k]) ^ place[ROW])
        for at, out in enumerate(outs):

            @pl.when(role == at)
            def _():
                y_copy(i, k, out).start()

    for k in range(n_h):
        h_copy(k).start()

    def start(i, _):
        w_copy(i).start()
        return _

    lax.fori_loop(0, chunks, start, 0)
    for k in range(n_h):
        h_copy(k).wait()

    def step(i, _):
        w_copy(i).wait()
        h = held[...].reshape(n_h * lanes, held.shape[2])
        held_y[i] = jnp.dot(h, held_w[i], preferred_element_type=F32).astype(BF16)
        for k in range(len(slots)):
            start_y(i, k)
        return _

    lax.fori_loop(0, chunks, step, 0)

    def finish(i, _):
        for k in range(len(slots)):
            y_copy(i, k, outs[0]).wait()
        return _

    lax.fori_loop(0, chunks, finish, 0)


def back_parts(place, slots, hs, w, chunks, prior=None, by_role=True):
    lanes, depth = hs[0].shape
    wide, n_h = w.shape[1], len(hs)
    block = pltpu.HBM((2 * lanes, wide), BF16)
    prior = list(prior or [])
    return pl.pallas_call(
        functools.partial(back_kernel, tuple(slots), by_role, len(prior), chunks),
        in_specs=[SMEM] + [ANY] * (n_h + 1 + len(prior)),
        out_specs=[ANY] * (4 if by_role else len(slots)),
        scratch_shapes=[
            pltpu.VMEM((n_h, lanes, depth), BF16),
            pltpu.VMEM((chunks, depth, wide // chunks), BF16),
            pltpu.VMEM((chunks, n_h * lanes, wide // chunks), BF16),
            DMA((n_h,)),
            DMA((chunks,)),
            DMA((chunks, len(slots))),
        ],
        out_shape=[block] * (4 if by_role else len(slots)),
        input_output_aliases={n_h + 2 + k: k for k in range(len(prior))},
        compiler_params=params(28),
        cost_estimate=cost(2 * n_h * lanes * depth * wide, 2 * wide * depth),
        name="back_parts",
    )(place, *in_hbm(*hs, w, *prior))


def weight_kernel(n_h, n_prior, place, own, *refs):
    got, hs, (grad, bias, held, sem) = refs[:3], refs[3 : 3 + n_h], refs[3 + n_h + n_prior :]

    @pl.when(pl.program_id(0) == 0)
    def _():
        for slot in range(n_h // 2):
            load_x(place, back_block(place, slot), own, got, held, 2 * slot, sem)
        for slot in range(n_h // 2):
            wait_x(own, held, 2 * slot, sem)

    lanes = held.shape[1]
    h = jnp.concatenate([ref[...] for ref in hs], axis=0)
    x = held[...].reshape(n_h * lanes, held.shape[2])
    grad[...] = lax.dot_general(h, x, (((0,), (0,)), ((), ())), preferred_element_type=F32)
    bias[...] = jnp.sum(h.astype(F32), axis=0, keepdims=True)


def weight_grads(place, own, got, hs, tile, first, count, prior=()):
    lanes, feats = hs[0].shape
    wide, n_h = own.shape[1], len(hs)
    return pl.pallas_call(
        functools.partial(weight_kernel, n_h, len(prior)),
        grid=(count,),
        in_specs=[SMEM]
        + [ANY] * 4
        + [pl.BlockSpec((lanes, tile), lambda i: (0, first + i))] * n_h
        + [ANY] * len(prior),
        out_specs=[pl.BlockSpec((tile, wide), lambda i: (first + i, 0)), pl.BlockSpec((1, tile), lambda i: (0, i))],
        scratch_shapes=[pltpu.VMEM((n_h, lanes, wide), BF16), DMA((n_h,))],
        out_shape=[pltpu.HBM((feats, wide), F32), jax.ShapeDtypeStruct((1, count * tile), F32)],
        input_output_aliases={5 + n_h + k: k for k in range(len(prior))},
        compiler_params=params(26),
        cost_estimate=cost(2 * n_h * lanes * wide * feats, 4 * wide * feats),
        name="weight_grads",
    )(place, *in_hbm(own, *got), *in_hbm(*hs), *in_hbm(*prior))


def wide_sum(*parts):
    parts = [jnp.concatenate(p, axis=1) if isinstance(p, list) else p for p in parts]
    return functools.reduce(lambda a, b: a + b, [p.astype(F32) for p in parts])


def add_kernel(*refs):
    q, others, out = refs[0], refs[1:-1], refs[-1]
    pieces, wide = others[-PIECES:], others[:-PIECES]
    run = pieces[0].shape[1]
    for k, piece in enumerate(pieces):
        part = pl.ds(k * run, run)
        total = q[:, part].astype(F32) + piece[...].astype(F32)
        for ref in wide:
            total += ref[:, part].astype(F32)
        out[:, part] = total.astype(out.dtype)


def add_parts(q, pieces, *more):
    return pl.pallas_call(
        add_kernel,
        in_specs=[VMEM] * (1 + len(more) + len(pieces)),
        out_specs=VMEM,
        out_shape=jax.ShapeDtypeStruct(q.shape, BF16),
        compiler_params=params(12),
        cost_estimate=cost(0, 0),
        name="add_parts",
    )(q, *more, *pieces)


def line_pairs(hops):
    return [(2 * a + core, 2 * b + core) for a, b in hops for core in (0, 1)]


def after(value, *done):
    return lax.optimization_barrier((value,) + done)[0]


def on_line(base_input, layer_input, out_grad, cross_weight, cross_bias):
    lanes = base_input.shape[0]
    col, row = lax.axis_index("col"), lax.axis_index("row")
    z, core = col // 2, col % 2
    end = jnp.logical_or(z == 0, z == 3)
    first = jnp.where(z < 2, 3, 0)
    place = jnp.stack([core, z, row, first, row ^ first]).astype(jnp.int32)

    def across(a, name):
        with jax.named_scope(name):
            return jax.tree.map(lambda one: lax.ppermute(one, "col", [(i, i ^ 1) for i in range(8)]), a)

    def line(a, hops, name):
        with jax.named_scope(name):
            return lax.ppermute(a, "col", line_pairs(hops))

    def plane(a, hops, name):
        pairs = [(8 * f + 2 * k + c, 8 * t + 2 * k + c) for k in range(4) for c, f, t in hops(k)]
        with jax.named_scope(name):
            return lax.ppermute(a, ("row", "col"), pairs)

    def first_way(k):
        return [(c, r, r ^ (1 + c)) for c in (0, 1) for r in range(4)]

    def second_way(k):
        return [(c, r, r ^ (2 - c)) for c in (0, 1) for r in range(4)]

    outer, inner = [(0, 1), (1, 0), (2, 3), (3, 2)], [(1, 2), (2, 1)]
    outwards, inwards = [(1, 0), (2, 3)], [(0, 1), (3, 2)]

    cross_weight = pltpu.with_memory_space_constraint(cross_weight, pltpu.VMEM)
    def pre(indices, got, *done):
        out = pre_parts(after(place, *done), layer_input, got, cross_weight, indices, 8)
        each = 1 + PIECES
        return [part for k in range(len(indices)) for part in (out[each * k], out[each * k + 1 : each * (k + 1)])]

    def back(slots, hs, *done, prior=None, by_role=True):
        return back_parts(after(place, *done), slots, hs, cross_weight, 8, prior, by_role)

    def both(*values, done):
        return lax.optimization_barrier(values + tuple(done))[: len(values)]

    relays = turned(place, place[REL]) == 1
    p1 = plane(layer_input, first_way, "p1")
    own_h = (out_grad.astype(F32) * base_input.astype(F32)).astype(BF16)
    a0, b0 = line(own_h, outer, "a0"), line(own_h, inner, "b0")
    h0 = across(own_h, "h0")
    to_p2 = jnp.where(relays, p1, layer_input)
    to_p3 = jnp.where(relays, layer_input, p1)
    p2 = plane(to_p2, second_way, "p2")
    roles = back((0,), (own_h, h0), to_p2, to_p3)

    a0, b0, p2, to_p3 = both(a0, b0, p2, to_p3, done=roles)
    a1, b1 = line(b0, outwards, "a1"), line(a0, inner, "b1")
    p3 = plane(to_p3, second_way, "p3")
    h1 = across(a0, "h1")
    q0, o0 = pre((0,), (p1, p2))
    o0 = across(o0, "o0")
    to_ra1 = add_parts(after(q0, p3), o0)
    ra1 = line(to_ra1, inwards, "ra1")
    q1, o1, q2, o2 = pre((1, 2), (p1, p2, p3), to_ra1)
    o1, o2 = across(o1, "o1"), across(o2, "o2")

    a1, b1 = both(a1, b1, done=(q1,))
    a2 = line(b1, outwards, "a2")
    s2 = jnp.where(end, a1, b0)
    h2 = across(s2, "h2")

    ra1, q0 = both(ra1, q0, done=(s2,))
    to_rb2, to_ra2 = add_parts(q0, o0, ra1), add_parts(q1, o1)
    rb2, ra2 = line(to_rb2, inner, "rb2"), line(to_ra2, inwards, "ra2")
    roles = back((1, 2), (a0, h1, s2, h2), to_rb2, to_ra2, *o2, prior=roles)

    a2, *roles = both(a2, *roles, done=())
    s3 = jnp.where(end, a2, b1)
    h3 = across(s3, "h3")
    e1, f1 = plane(roles[1], first_way, "e1"), plane(roles[3], first_way, "f1")
    rb2, ra2 = both(rb2, ra2, done=(s3,))
    (part,) = back((3,), (s3, h3), roles[0], rb2, ra2, by_role=False)

    rb2, ra2 = both(rb2, ra2, done=(part,))
    to_ra3, to_rb3 = add_parts(q2, o2, rb2), add_parts(q1, o1, ra2)
    ra3, rb3 = line(to_ra3, outer, "ra3"), line(to_rb3, inner, "rb3")

    mine, relayed = roles[0], roles[2]
    last_of = [3, 3, 0, 0]

    def last_first(k):
        return [(0, f ^ last_of[k], t ^ last_of[k]) for f, t in ((3, 2), (1, 0))] + [
            (1, f ^ last_of[k], t ^ last_of[k]) for f, t in ((3, 1), (2, 0))
        ]

    def last_second(k):
        return [(0, 2 ^ last_of[k], last_of[k]), (1, 1 ^ last_of[k], last_of[k])]

    l1 = plane(part, last_first, "l1")
    f1, e1 = both(f1, e1, done=(part,))
    to_e2 = wide_sum(relayed, f1).astype(BF16)
    e2 = plane(to_e2, second_way, "e2")
    q3, o3 = pre((3,), (p1, p2, p3), to_e2, to_ra3, to_rb3)
    o3 = across(o3, "o3")
    to_l2 = wide_sum(part, after(l1, q3)).astype(BF16)
    l2 = plane(to_l2, last_second, "l2")
    hs = (own_h, h0, a0, h1, s2, h2, s3, h3)
    grad, bias = weight_grads(after(place, to_l2), layer_input, (p1, p2, p3), hs, 512, 0, base_input.shape[1] // 512)
    ra3, rb3, *o3 = both(ra3, rb3, *o3, done=(bias,))
    preact = wide_sum(ra3, rb3, q3, o3) + cross_bias.astype(F32)[None, :]
    base_grad = (out_grad.astype(F32) * preact).astype(BF16)
    l2, e2 = both(l2, e2, done=(base_grad,))
    branch = jnp.where(row == back_block(place, 3), wide_sum(to_l2, l2), wide_sum(mine, e1, e2)).astype(BF16)
    return (grad, bias[0], base_grad, branch)


def on_any(base_input, layer_input, out_grad, cross_weight, cross_bias):
    input_panel = lax.all_gather(layer_input, "row", axis=0, tiled=True)
    hidden = (out_grad.astype(F32) * base_input.astype(F32)).astype(BF16)
    hidden_panel = lax.all_gather(hidden, "col", axis=0, tiled=True)
    weight_grad = lax.dot_general(
        hidden_panel, input_panel, (((0,), (0,)), ((), ())), preferred_element_type=F32
    )
    bias_grad = jnp.sum(hidden_panel, axis=0, dtype=F32)
    part = lax.dot_general(input_panel, cross_weight, (((1,), (1,)), ((), ())), preferred_element_type=F32)
    preact = lax.psum_scatter(part.astype(BF16), "col", scatter_dimension=0, tiled=True).astype(F32)
    preact = preact + cross_bias.astype(F32)[None, :]
    base_grad = (out_grad.astype(F32) * preact).astype(BF16)
    part = jnp.dot(hidden_panel, cross_weight, preferred_element_type=F32).astype(BF16)
    branch = lax.psum_scatter(part, "row", scatter_dimension=0, tiled=True)
    return (weight_grad, bias_grad, base_grad, branch)


def solution(mesh):
    in_specs = (P("col", "row"), P("row", "col"), P("col", "row"), P("row", "col"), P("row"))
    out_specs = (P("row", "col"), P("row"), P("col", "row"), P("row", "col"))
    body = on_line if (mesh.shape["row"], mesh.shape["col"]) == (4, 8) else on_any
    return jax.shard_map(body, mesh=mesh, in_specs=in_specs, out_specs=out_specs, check_vma=False)
```

```python
import functools

import jax
import jax.numpy as jnp
from jax import lax
from jax.experimental import pallas as pl
from jax.experimental.pallas import tpu as pltpu
from jax.sharding import PartitionSpec as P

F32, BF16 = jnp.float32, jnp.bfloat16
ANY = pl.BlockSpec(memory_space=pl.ANY)
SMEM = pl.BlockSpec(memory_space=pltpu.SMEM)
VMEM = pl.BlockSpec(memory_space=pltpu.VMEM)
DMA = pltpu.SemaphoreType.DMA
MIB = 1024 * 1024

CORE, Z, ROW, FIRST, REL = range(5)
PIECES = 2


def params(mib):
    return pltpu.CompilerParams(vmem_limit_bytes=mib * MIB)


def in_hbm(*arrays):
    return [pltpu.with_memory_space_constraint(a, pltpu.HBM) for a in arrays]


def cost(flops, nbytes):
    return pl.CostEstimate(flops=1, bytes_accessed=1, transcendentals=0)


def turned(place, apart):
    other = jnp.where(apart == 1, 2, jnp.where(apart == 2, 1, apart))
    return jnp.where(place[CORE] == 0, apart, other)


def x_sources(place, block, half, own, got):
    lanes = own.shape[0] // 2
    apart = turned(place, block ^ place[ROW])
    last = place[REL] == 3
    conds = [apart == 0, apart == 1]
    conds.append(jnp.where(last, apart == 3, apart == 2))
    conds.append(jnp.where(last, apart == 2, apart == 3))
    refs = (own,) + tuple(got)
    return [(ref.at[pl.ds(half * lanes, lanes)], cond) for ref, cond in zip(refs, conds) if ref is not None]


def load_x(place, block, own, got, held, at, sem):
    for half in range(2):
        slot = at + jnp.where(place[CORE] == half, 0, 1)
        for ref, cond in x_sources(place, block, half, own, got):

            @pl.when(cond)
            def _():
                pltpu.make_async_copy(ref, held.at[slot], sem.at[slot]).start()


def wait_x(own, held, at, sem):
    lanes = own.shape[0] // 2
    for k in (at, at + 1):
        pltpu.make_async_copy(own.at[pl.ds(0, lanes)], held.at[k], sem.at[k]).wait()


def pre_block(place, index):
    middle = jnp.logical_or(place[Z] == 1, place[Z] == 2)
    swapped = jnp.where(index == 2, 3, jnp.where(index == 3, 2, index))
    return jnp.where(middle, swapped, index) ^ place[FIRST]


def pre_order(place):
    middle = jnp.logical_or(place[Z] == 1, place[Z] == 2)
    rel = place[REL]
    own = jnp.where(middle, jnp.where(rel == 2, 3, jnp.where(rel == 3, 2, rel)), rel)
    return own, jnp.where(own == 0, 1, 0), jnp.where(own <= 1, 2, 1), jnp.where(own == 3, 2, 3)


def back_block(place, slot):
    low = place[Z] < 2
    return (place[Z], place[Z] ^ 1, jnp.where(low, 2, 1), jnp.where(low, 3, 0))[slot]


def pre_kernel(turns, slots, n_got, n_prior, chunks, place, own, *refs):
    got = list(refs[:n_got]) + [None] * (3 - n_got)
    w, refs = refs[n_got], refs[n_got + 1 + n_prior :]
    outs, (held, held_w, held_y, sem, sem_w, sem_y) = refs[:-6], refs[-6:]
    lanes = held.shape[1]
    tile = w.shape[0] // chunks
    run = chunks // PIECES
    order = pre_order(place)

    def w_copy(i):
        part = pl.ds(pl.multiple_of(i * tile, tile), tile)
        return pltpu.make_async_copy(w.at[part], held_w.at[part], sem_w.at[i])

    def y_copy(i, k, out, at):
        part = pl.ds(pl.multiple_of(at * tile, tile), tile)
        return pltpu.make_async_copy(held_y.at[i, pl.ds(k * lanes, lanes)], out.at[:, part], sem_y.at[i, k])

    def start_y(i):
        for b, turn in enumerate(turns):
            for at, slot in enumerate(slots):
                mine, *other = outs[(1 + PIECES) * at : (1 + PIECES) * (at + 1)]

                @pl.when(order[turn] == slot)
                def _():
                    y_copy(i, 2 * b, mine, i).start()

                for piece, out in enumerate(other):

                    @pl.when(jnp.logical_and(order[turn] == slot, i // run == piece))
                    def _():
                        y_copy(i, 2 * b + 1, out, i % run).start()

    for b, turn in enumerate(turns):
        load_x(place, pre_block(place, order[turn]), own, got, held, 2 * b, sem)

    def start(i, _):
        w_copy(i).start()
        return _

    lax.fori_loop(0, chunks, start, 0)
    for b in range(len(turns)):
        wait_x(own, held, 2 * b, sem)

    def step(i, _):
        w_copy(i).wait()
        x = held[...].reshape(2 * len(turns) * lanes, held.shape[2])
        rows = held_w[pl.ds(pl.multiple_of(i * tile, tile), tile)]
        held_y[i] = lax.dot_general(x, rows, (((1,), (1,)), ((), ())), preferred_element_type=F32).astype(BF16)
        start_y(i)
        return _

    lax.fori_loop(0, chunks, step, 0)

    def finish(i, _):
        for k in range(2 * len(turns)):
            y_copy(i, k, outs[0], 0).wait()
        return _

    lax.fori_loop(0, chunks, finish, 0)


def pre_parts(place, own, got, w, turns, slots, chunks, prior=()):
    rows, depth = own.shape
    lanes, wide, parts = rows // 2, w.shape[0], 2 * len(turns)
    return pl.pallas_call(
        functools.partial(pre_kernel, turns, slots, len(got), len(prior), chunks),
        in_specs=[SMEM] + [ANY] * (2 + len(got) + len(prior)),
        out_specs=[ANY] * ((1 + PIECES) * len(slots)),
        scratch_shapes=[
            pltpu.VMEM((parts, lanes, depth), BF16),
            pltpu.VMEM((wide, depth), BF16),
            pltpu.VMEM((chunks, parts * lanes, wide // chunks), BF16),
            DMA((parts,)),
            DMA((chunks,)),
            DMA((chunks, parts)),
        ],
        out_shape=[pltpu.HBM((lanes, n), BF16) for n in [wide] + [wide // PIECES] * PIECES] * len(slots),
        input_output_aliases={3 + len(got) + k: k for k in range(len(prior))},
        compiler_params=params(28),
        cost_estimate=cost(2 * parts * lanes * depth * wide, 2 * wide * depth),
        name="pre_parts",
    )(place, *in_hbm(own, *got, w, *prior))


def back_kernel(slots, by_role, n_prior, chunks, place, *refs):
    n_h = 2 * len(slots)
    hs, w, refs = refs[:n_h], refs[n_h], refs[n_h + 1 + n_prior :]
    outs, (held, held_w, held_y, sem, sem_w, sem_y) = refs[:-6], refs[-6:]
    lanes = held.shape[1]
    tile = w.shape[1] // chunks

    def w_copy(i):
        part = pl.ds(pl.multiple_of(i * tile, tile), tile)
        return pltpu.make_async_copy(w.at[:, part], held_w.at[i], sem_w.at[i])

    def h_copy(k):
        slot = k // 2 * 2 + (place[CORE] if k % 2 == 0 else 1 - place[CORE])
        return pltpu.make_async_copy(hs[k], held.at[slot], sem.at[k])

    def y_copy(i, k, out):
        part = pl.ds(pl.multiple_of(i * tile, tile), tile)
        return pltpu.make_async_copy(held_y.at[i, pl.ds(2 * k * lanes, 2 * lanes)], out.at[:, part], sem_y.at[i, k])

    def start_y(i, k):
        if not by_role:
            y_copy(i, k, outs[k]).start()
            return
        role = turned(place, back_block(place, slots[k]) ^ place[ROW])
        for at, out in enumerate(outs):

            @pl.when(role == at)
            def _():
                y_copy(i, k, out).start()

    for k in range(n_h):
        h_copy(k).start()

    def start(i, _):
        w_copy(i).start()
        return _

    lax.fori_loop(0, chunks, start, 0)
    for k in range(n_h):
        h_copy(k).wait()

    def step(i, _):
        w_copy(i).wait()
        h = held[...].reshape(n_h * lanes, held.shape[2])
        held_y[i] = jnp.dot(h, held_w[i], preferred_element_type=F32).astype(BF16)
        for k in range(len(slots)):
            start_y(i, k)
        return _

    lax.fori_loop(0, chunks, step, 0)

    def finish(i, _):
        for k in range(len(slots)):
            y_copy(i, k, outs[0]).wait()
        return _

    lax.fori_loop(0, chunks, finish, 0)


def back_parts(place, slots, hs, w, chunks, prior=None, by_role=True):
    lanes, depth = hs[0].shape
    wide, n_h = w.shape[1], len(hs)
    block = pltpu.HBM((2 * lanes, wide), BF16)
    prior = list(prior or [])
    return pl.pallas_call(
        functools.partial(back_kernel, tuple(slots), by_role, len(prior), chunks),
        in_specs=[SMEM] + [ANY] * (n_h + 1 + len(prior)),
        out_specs=[ANY] * (4 if by_role else len(slots)),
        scratch_shapes=[
            pltpu.VMEM((n_h, lanes, depth), BF16),
            pltpu.VMEM((chunks, depth, wide // chunks), BF16),
            pltpu.VMEM((chunks, n_h * lanes, wide // chunks), BF16),
            DMA((n_h,)),
            DMA((chunks,)),
            DMA((chunks, len(slots))),
        ],
        out_shape=[block] * (4 if by_role else len(slots)),
        input_output_aliases={n_h + 2 + k: k for k in range(len(prior))},
        compiler_params=params(28),
        cost_estimate=cost(2 * n_h * lanes * depth * wide, 2 * wide * depth),
        name="back_parts",
    )(place, *in_hbm(*hs, w, *prior))


def weight_kernel(n_h, n_prior, place, own, *refs):
    got, hs, (grad, bias, held, sem) = refs[:3], refs[3 : 3 + n_h], refs[3 + n_h + n_prior :]

    @pl.when(pl.program_id(0) == 0)
    def _():
        for slot in range(n_h // 2):
            load_x(place, back_block(place, slot), own, got, held, 2 * slot, sem)
        for slot in range(n_h // 2):
            wait_x(own, held, 2 * slot, sem)

    lanes = held.shape[1]
    h = jnp.concatenate([ref[...] for ref in hs], axis=0)
    x = held[...].reshape(n_h * lanes, held.shape[2])
    grad[...] = lax.dot_general(h, x, (((0,), (0,)), ((), ())), preferred_element_type=F32)
    bias[...] = jnp.sum(h.astype(F32), axis=0, keepdims=True)


def weight_grads(place, own, got, hs, tile, first, count, prior=()):
    lanes, feats = hs[0].shape
    wide, n_h = own.shape[1], len(hs)
    return pl.pallas_call(
        functools.partial(weight_kernel, n_h, len(prior)),
        grid=(count,),
        in_specs=[SMEM]
        + [ANY] * 4
        + [pl.BlockSpec((lanes, tile), lambda i: (0, first + i))] * n_h
        + [ANY] * len(prior),
        out_specs=[pl.BlockSpec((tile, wide), lambda i: (first + i, 0)), pl.BlockSpec((1, tile), lambda i: (0, first + i))],
        scratch_shapes=[pltpu.VMEM((n_h, lanes, wide), BF16), DMA((n_h,))],
        out_shape=[pltpu.HBM((feats, wide), F32), pltpu.HBM((1, feats), F32)],
        input_output_aliases={5 + n_h + k: k for k in range(len(prior))},
        compiler_params=params(26),
        cost_estimate=cost(2 * n_h * lanes * wide * feats, 4 * wide * feats),
        name="weight_grads",
    )(place, *in_hbm(own, *got), *in_hbm(*hs), *in_hbm(*prior))


def wide_sum(*parts):
    parts = [jnp.concatenate(p, axis=1) if isinstance(p, list) else p for p in parts]
    return functools.reduce(lambda a, b: a + b, [p.astype(F32) for p in parts])


def add_kernel(*refs):
    q, others, out = refs[0], refs[1:-1], refs[-1]
    pieces, wide = others[-PIECES:], others[:-PIECES]
    run = pieces[0].shape[1]
    for k, piece in enumerate(pieces):
        part = pl.ds(k * run, run)
        total = q[:, part].astype(F32) + piece[...].astype(F32)
        for ref in wide:
            total += ref[:, part].astype(F32)
        out[:, part] = total.astype(out.dtype)


def add_parts(q, pieces, *more):
    return pl.pallas_call(
        add_kernel,
        in_specs=[VMEM] * (1 + len(more) + len(pieces)),
        out_specs=VMEM,
        out_shape=jax.ShapeDtypeStruct(q.shape, BF16),
        compiler_params=params(12),
        cost_estimate=cost(0, 0),
        name="add_parts",
    )(q, *more, *pieces)


def pair_kernel(a, b, out):
    out[...] = (a[...].astype(F32) + b[...].astype(F32)).astype(out.dtype)


def add_pair(a, b):
    return pl.pallas_call(
        pair_kernel,
        in_specs=[VMEM] * 2,
        out_specs=VMEM,
        out_shape=jax.ShapeDtypeStruct(a.shape, BF16),
        compiler_params=params(8),
        cost_estimate=cost(0, 0),
        name="add_pair",
    )(a, b)


def base_kernel(grad, bias, q, *refs):
    pieces, wide, out = refs[:PIECES], refs[PIECES:-1], refs[-1]
    run = pieces[0].shape[1]
    for k, piece in enumerate(pieces):
        part = pl.ds(k * run, run)
        total = q[:, part].astype(F32) + piece[...].astype(F32)
        for ref in wide:
            total += ref[:, part].astype(F32)
        total += bias[:, part].astype(F32)
        out[:, part] = (grad[:, part].astype(F32) * total).astype(out.dtype)


def base_grads(grad, bias, q, pieces, *more):
    return pl.pallas_call(
        base_kernel,
        in_specs=[VMEM] * (3 + len(pieces) + len(more)),
        out_specs=VMEM,
        out_shape=jax.ShapeDtypeStruct(grad.shape, BF16),
        compiler_params=params(16),
        cost_estimate=pl.CostEstimate(flops=1, bytes_accessed=grad.size, transcendentals=0),
        name="base_grads",
    )(grad, bias[None, :], q, *pieces, *more)


def line_pairs(hops):
    return [(2 * a + core, 2 * b + core) for a, b in hops for core in (0, 1)]


def after(value, *done):
    return lax.optimization_barrier((value,) + done)[0]


def on_line(base_input, layer_input, out_grad, cross_weight, cross_bias):
    lanes = base_input.shape[0]
    col, row = lax.axis_index("col"), lax.axis_index("row")
    z, core = col // 2, col % 2
    end = jnp.logical_or(z == 0, z == 3)
    first = jnp.where(z < 2, 3, 0)
    place = jnp.stack([core, z, row, first, row ^ first]).astype(jnp.int32)

    def across(a, name):
        with jax.named_scope(name):
            return jax.tree.map(lambda one: lax.ppermute(one, "col", [(i, i ^ 1) for i in range(8)]), a)

    def line(a, hops, name):
        with jax.named_scope(name):
            return lax.ppermute(a, "col", line_pairs(hops))

    def plane(a, hops, name):
        pairs = [(8 * f + 2 * k + c, 8 * t + 2 * k + c) for k in range(4) for c, f, t in hops(k)]
        with jax.named_scope(name):
            return lax.ppermute(a, ("row", "col"), pairs)

    def first_way(k):
        return [(c, r, r ^ (1 + c)) for c in (0, 1) for r in range(4)]

    def second_way(k):
        return [(c, r, r ^ (2 - c)) for c in (0, 1) for r in range(4)]

    outer, inner = [(0, 1), (1, 0), (2, 3), (3, 2)], [(1, 2), (2, 1)]
    outwards, inwards = [(1, 0), (2, 3)], [(0, 1), (3, 2)]

    cross_weight = pltpu.with_memory_space_constraint(cross_weight, pltpu.VMEM)
    def pre(turns, slots, got, *done, prior=()):
        return list(pre_parts(after(place, *done), layer_input, got, cross_weight, turns, slots, 8, prior))

    def back(slots, hs, *done, prior=None, by_role=True):
        return back_parts(after(place, *done), slots, hs, cross_weight, 8, prior, by_role)

    def both(*values, done):
        return lax.optimization_barrier(values + tuple(done))[: len(values)]

    relays = turned(place, place[REL]) == 1
    p1 = plane(layer_input, first_way, "p1")
    own_h = (out_grad.astype(F32) * base_input.astype(F32)).astype(BF16)
    a0, b0 = line(own_h, outer, "a0"), line(own_h, inner, "b0")
    h0 = across(own_h, "h0")
    each = 1 + PIECES
    q = pre((0,), (0, 1, 2, 3), (), own_h)
    p1 = after(p1, q[0])
    to_p2 = jnp.where(relays, p1, layer_input)
    to_p3 = jnp.where(relays, layer_input, p1)
    p2 = plane(to_p2, second_way, "p2")
    roles = back((0,), (own_h, h0), to_p2, to_p3)

    a0, b0, p2, to_p3 = both(a0, b0, p2, to_p3, done=roles)
    a1, b1 = line(b0, outwards, "a1"), line(a0, inner, "b1")
    p3 = plane(to_p3, second_way, "p3")
    h1 = across(a0, "h1")
    q[: 2 * each] = pre((1,), (0, 1), (p1, p2), prior=q[: 2 * each])
    q0, o0 = q[0], across(q[1:each], "o0")
    to_ra1 = add_parts(after(q0, p3), o0)
    ra1 = line(to_ra1, inwards, "ra1")
    q[each:] = pre((2, 3), (1, 2, 3), (p1, p2, p3), to_ra1, prior=q[each:])
    q1, q2, q3 = q[each], q[2 * each], q[3 * each]
    o1, o2, o3 = [across(q[k * each + 1 : (k + 1) * each], f"o{k}") for k in (1, 2, 3)]

    a1, b1 = both(a1, b1, done=(q1,))
    a2 = line(b1, outwards, "a2")
    s2 = jnp.where(end, a1, b0)
    h2 = across(s2, "h2")

    ra1, q0 = both(ra1, q0, done=(s2,))
    to_rb2, to_ra2 = add_parts(q0, o0, ra1), add_parts(q1, o1)
    rb2, ra2 = line(to_rb2, inner, "rb2"), line(to_ra2, inwards, "ra2")
    roles = back((1, 2), (a0, h1, s2, h2), to_rb2, to_ra2, *o2, prior=roles)

    a2, *roles = both(a2, *roles, done=())
    s3 = jnp.where(end, a2, b1)
    h3 = across(s3, "h3")
    rb2, ra2 = both(rb2, ra2, done=(s3,))
    mine, near, relayed, far = back((3,), (s3, h3), rb2, ra2, prior=roles)

    rb2, ra2 = both(rb2, ra2, done=(far,))
    to_ra3, to_rb3 = add_parts(q2, o2, rb2), add_parts(q1, o1, ra2)
    ra3, rb3 = line(to_ra3, outer, "ra3"), line(to_rb3, inner, "rb3")

    f1, e1 = plane(far, first_way, "f1"), plane(near, first_way, "e1")
    hs = (own_h, h0, a0, h1, s2, h2, s3, h3)
    tile = 512
    tiles = base_input.shape[1] // tile
    early = tiles * 3 // 4
    got = (p1, p2, p3)
    grads = weight_grads(after(place, to_ra3, to_rb3), layer_input, got, hs, tile, 0, early)
    to_e2 = add_pair(relayed, after(f1, *grads))
    e2 = plane(to_e2, second_way, "e2")
    grad, bias = weight_grads(after(place, to_e2), layer_input, got, hs, tile, early, tiles - early, grads)
    ra3, rb3, e1, *o3 = both(ra3, rb3, e1, *o3, done=(bias,))
    base_grad = base_grads(out_grad, cross_bias, q3, o3, ra3, rb3)
    branch = wide_sum(mine, e1, after(e2, base_grad)).astype(BF16)
    return (grad, bias[0], base_grad, branch)


def on_any(base_input, layer_input, out_grad, cross_weight, cross_bias):
    input_panel = lax.all_gather(layer_input, "row", axis=0, tiled=True)
    hidden = (out_grad.astype(F32) * base_input.astype(F32)).astype(BF16)
    hidden_panel = lax.all_gather(hidden, "col", axis=0, tiled=True)
    weight_grad = lax.dot_general(
        hidden_panel, input_panel, (((0,), (0,)), ((), ())), preferred_element_type=F32
    )
    bias_grad = jnp.sum(hidden_panel, axis=0, dtype=F32)
    part = lax.dot_general(input_panel, cross_weight, (((1,), (1,)), ((), ())), preferred_element_type=F32)
    preact = lax.psum_scatter(part.astype(BF16), "col", scatter_dimension=0, tiled=True).astype(F32)
    preact = preact + cross_bias.astype(F32)[None, :]
    base_grad = (out_grad.astype(F32) * preact).astype(BF16)
    part = jnp.dot(hidden_panel, cross_weight, preferred_element_type=F32).astype(BF16)
    branch = lax.psum_scatter(part, "row", scatter_dimension=0, tiled=True)
    return (weight_grad, bias_grad, base_grad, branch)


def solution(mesh):
    in_specs = (P("col", "row"), P("row", "col"), P("col", "row"), P("row", "col"), P("row"))
    out_specs = (P("row", "col"), P("row"), P("col", "row"), P("row", "col"))
    body = on_line if (mesh.shape["row"], mesh.shape["col"]) == (4, 8) else on_any
    return jax.shard_map(body, mesh=mesh, in_specs=in_specs, out_specs=out_specs, check_vma=False)
```

```python
import functools

import jax
import jax.numpy as jnp
from jax import lax
from jax.experimental import pallas as pl
from jax.experimental.pallas import tpu as pltpu
from jax.sharding import PartitionSpec as P

F32, BF16 = jnp.float32, jnp.bfloat16
ANY = pl.BlockSpec(memory_space=pl.ANY)
SMEM = pl.BlockSpec(memory_space=pltpu.SMEM)
VMEM = pl.BlockSpec(memory_space=pltpu.VMEM)
DMA = pltpu.SemaphoreType.DMA
MIB = 1024 * 1024

CORE, Z, ROW, FIRST, REL = range(5)
PIECES = 2


def params(mib):
    return pltpu.CompilerParams(vmem_limit_bytes=mib * MIB)


def in_hbm(*arrays):
    return [pltpu.with_memory_space_constraint(a, pltpu.HBM) for a in arrays]


def cost(flops, nbytes):
    return pl.CostEstimate(flops=1, bytes_accessed=1, transcendentals=0)


def turned(place, apart):
    other = jnp.where(apart == 1, 2, jnp.where(apart == 2, 1, apart))
    return jnp.where(place[CORE] == 0, apart, other)


def x_sources(place, block, half, own, got):
    lanes = own.shape[0] // 2
    apart = turned(place, block ^ place[ROW])
    last = place[REL] == 3
    conds = [apart == 0, apart == 1]
    conds.append(jnp.where(last, apart == 3, apart == 2))
    conds.append(jnp.where(last, apart == 2, apart == 3))
    refs = (own,) + tuple(got)
    return [(ref.at[pl.ds(half * lanes, lanes)], cond) for ref, cond in zip(refs, conds) if ref is not None]


def load_x(place, block, own, got, held, at, sem):
    for half in range(2):
        slot = at + jnp.where(place[CORE] == half, 0, 1)
        for ref, cond in x_sources(place, block, half, own, got):

            @pl.when(cond)
            def _():
                pltpu.make_async_copy(ref, held.at[slot], sem.at[slot]).start()


def wait_x(own, held, at, sem):
    lanes = own.shape[0] // 2
    for k in (at, at + 1):
        pltpu.make_async_copy(own.at[pl.ds(0, lanes)], held.at[k], sem.at[k]).wait()


def pre_block(place, index):
    middle = jnp.logical_or(place[Z] == 1, place[Z] == 2)
    swapped = jnp.where(index == 2, 3, jnp.where(index == 3, 2, index))
    return jnp.where(middle, swapped, index) ^ place[FIRST]


def pre_order(place):
    middle = jnp.logical_or(place[Z] == 1, place[Z] == 2)
    rel = place[REL]
    own = jnp.where(middle, jnp.where(rel == 2, 3, jnp.where(rel == 3, 2, rel)), rel)
    return own, jnp.where(own == 0, 1, 0), jnp.where(own <= 1, 2, 1), jnp.where(own == 3, 2, 3)


def back_block(place, slot):
    low = place[Z] < 2
    return (place[Z], place[Z] ^ 1, jnp.where(low, 2, 1), jnp.where(low, 3, 0))[slot]


def pre_kernel(turns, slots, n_got, n_prior, chunks, place, own, *refs):
    got = list(refs[:n_got]) + [None] * (3 - n_got)
    w, refs = refs[n_got], refs[n_got + 1 + n_prior :]
    outs, (held, held_w, held_y, sem, sem_w, sem_y) = refs[:-6], refs[-6:]
    lanes = held.shape[1]
    tile = w.shape[0] // chunks
    run = chunks // PIECES
    order = pre_order(place)

    def w_copy(i):
        part = pl.ds(pl.multiple_of(i * tile, tile), tile)
        return pltpu.make_async_copy(w.at[part], held_w.at[part], sem_w.at[i])

    def y_copy(i, k, out, at):
        part = pl.ds(pl.multiple_of(at * tile, tile), tile)
        return pltpu.make_async_copy(held_y.at[i, pl.ds(k * lanes, lanes)], out.at[:, part], sem_y.at[i, k])

    def start_y(i):
        for b, turn in enumerate(turns):
            for at, slot in enumerate(slots):
                mine, *other = outs[(1 + PIECES) * at : (1 + PIECES) * (at + 1)]

                @pl.when(order[turn] == slot)
                def _():
                    y_copy(i, 2 * b, mine, i).start()

                for piece, out in enumerate(other):

                    @pl.when(jnp.logical_and(order[turn] == slot, i // run == piece))
                    def _():
                        y_copy(i, 2 * b + 1, out, i % run).start()

    for b, turn in enumerate(turns):
        load_x(place, pre_block(place, order[turn]), own, got, held, 2 * b, sem)

    def start(i, _):
        w_copy(i).start()
        return _

    lax.fori_loop(0, chunks, start, 0)
    for b in range(len(turns)):
        wait_x(own, held, 2 * b, sem)

    def step(i, _):
        w_copy(i).wait()
        x = held[...].reshape(2 * len(turns) * lanes, held.shape[2])
        rows = held_w[pl.ds(pl.multiple_of(i * tile, tile), tile)]
        held_y[i] = lax.dot_general(x, rows, (((1,), (1,)), ((), ())), preferred_element_type=F32).astype(BF16)
        start_y(i)
        return _

    lax.fori_loop(0, chunks, step, 0)

    def finish(i, _):
        for k in range(2 * len(turns)):
            y_copy(i, k, outs[0], 0).wait()
        return _

    lax.fori_loop(0, chunks, finish, 0)


def pre_parts(place, own, got, w, turns, slots, chunks, prior=()):
    rows, depth = own.shape
    lanes, wide, parts = rows // 2, w.shape[0], 2 * len(turns)
    return pl.pallas_call(
        functools.partial(pre_kernel, turns, slots, len(got), len(prior), chunks),
        in_specs=[SMEM] + [ANY] * (2 + len(got) + len(prior)),
        out_specs=[ANY] * ((1 + PIECES) * len(slots)),
        scratch_shapes=[
            pltpu.VMEM((parts, lanes, depth), BF16),
            pltpu.VMEM((wide, depth), BF16),
            pltpu.VMEM((chunks, parts * lanes, wide // chunks), BF16),
            DMA((parts,)),
            DMA((chunks,)),
            DMA((chunks, parts)),
        ],
        out_shape=[pltpu.HBM((lanes, n), BF16) for n in [wide] + [wide // PIECES] * PIECES] * len(slots),
        input_output_aliases={3 + len(got) + k: k for k in range(len(prior))},
        compiler_params=params(28),
        cost_estimate=cost(2 * parts * lanes * depth * wide, 2 * wide * depth),
        name="pre_parts",
    )(place, *in_hbm(own, *got, w, *prior))


def back_kernel(slots, by_role, n_prior, chunks, place, *refs):
    n_h = 2 * len(slots)
    hs, w, refs = refs[:n_h], refs[n_h], refs[n_h + 1 + n_prior :]
    outs, (held, held_w, held_y, sem, sem_w, sem_y) = refs[:-6], refs[-6:]
    lanes = held.shape[1]
    tile = w.shape[1] // chunks

    def w_copy(i):
        part = pl.ds(pl.multiple_of(i * tile, tile), tile)
        return pltpu.make_async_copy(w.at[:, part], held_w.at[i], sem_w.at[i])

    def h_copy(k):
        slot = k // 2 * 2 + (place[CORE] if k % 2 == 0 else 1 - place[CORE])
        return pltpu.make_async_copy(hs[k], held.at[slot], sem.at[k])

    def y_copy(i, k, out):
        part = pl.ds(pl.multiple_of(i * tile, tile), tile)
        return pltpu.make_async_copy(held_y.at[i, pl.ds(2 * k * lanes, 2 * lanes)], out.at[:, part], sem_y.at[i, k])

    def start_y(i, k):
        if not by_role:
            y_copy(i, k, outs[k]).start()
            return
        role = turned(place, back_block(place, slots[k]) ^ place[ROW])
        for at, out in enumerate(outs):

            @pl.when(role == at)
            def _():
                y_copy(i, k, out).start()

    for k in range(n_h):
        h_copy(k).start()

    def start(i, _):
        w_copy(i).start()
        return _

    lax.fori_loop(0, chunks, start, 0)
    for k in range(n_h):
        h_copy(k).wait()

    def step(i, _):
        w_copy(i).wait()
        h = held[...].reshape(n_h * lanes, held.shape[2])
        held_y[i] = jnp.dot(h, held_w[i], preferred_element_type=F32).astype(BF16)
        for k in range(len(slots)):
            start_y(i, k)
        return _

    lax.fori_loop(0, chunks, step, 0)

    def finish(i, _):
        for k in range(len(slots)):
            y_copy(i, k, outs[0]).wait()
        return _

    lax.fori_loop(0, chunks, finish, 0)


def back_parts(place, slots, hs, w, chunks, prior=None, by_role=True):
    lanes, depth = hs[0].shape
    wide, n_h = w.shape[1], len(hs)
    block = pltpu.HBM((2 * lanes, wide), BF16)
    prior = list(prior or [])
    return pl.pallas_call(
        functools.partial(back_kernel, tuple(slots), by_role, len(prior), chunks),
        in_specs=[SMEM] + [ANY] * (n_h + 1 + len(prior)),
        out_specs=[ANY] * (4 if by_role else len(slots)),
        scratch_shapes=[
            pltpu.VMEM((n_h, lanes, depth), BF16),
            pltpu.VMEM((chunks, depth, wide // chunks), BF16),
            pltpu.VMEM((chunks, n_h * lanes, wide // chunks), BF16),
            DMA((n_h,)),
            DMA((chunks,)),
            DMA((chunks, len(slots))),
        ],
        out_shape=[block] * (4 if by_role else len(slots)),
        input_output_aliases={n_h + 2 + k: k for k in range(len(prior))},
        compiler_params=params(28),
        cost_estimate=cost(2 * n_h * lanes * depth * wide, 2 * wide * depth),
        name="back_parts",
    )(place, *hs, *in_hbm(w, *prior))


def weight_kernel(n_h, n_prior, place, own, *refs):
    got, hs, (grad, bias, held, sem) = refs[:3], refs[3 : 3 + n_h], refs[3 + n_h + n_prior :]

    @pl.when(pl.program_id(0) == 0)
    def _():
        for slot in range(n_h // 2):
            load_x(place, back_block(place, slot), own, got, held, 2 * slot, sem)
        for slot in range(n_h // 2):
            wait_x(own, held, 2 * slot, sem)

    lanes = held.shape[1]
    h = jnp.concatenate([ref[...] for ref in hs], axis=0)
    x = held[...].reshape(n_h * lanes, held.shape[2])
    grad[...] = lax.dot_general(h, x, (((0,), (0,)), ((), ())), preferred_element_type=F32)
    bias[...] = jnp.sum(h.astype(F32), axis=0, keepdims=True)


def weight_grads(place, own, got, hs, tile, first, count, prior=()):
    lanes, feats = hs[0].shape
    wide, n_h = own.shape[1], len(hs)
    return pl.pallas_call(
        functools.partial(weight_kernel, n_h, len(prior)),
        grid=(count,),
        in_specs=[SMEM]
        + [ANY] * 4
        + [pl.BlockSpec((lanes, tile), lambda i: (0, first + i))] * n_h
        + [ANY] * len(prior),
        out_specs=[pl.BlockSpec((tile, wide), lambda i: (first + i, 0)), pl.BlockSpec((1, tile), lambda i: (0, first + i))],
        scratch_shapes=[pltpu.VMEM((n_h, lanes, wide), BF16), DMA((n_h,))],
        out_shape=[pltpu.HBM((feats, wide), F32), pltpu.HBM((1, feats), F32)],
        input_output_aliases={5 + n_h + k: k for k in range(len(prior))},
        compiler_params=params(26),
        cost_estimate=cost(2 * n_h * lanes * wide * feats, 4 * wide * feats),
        name="weight_grads",
    )(place, *in_hbm(own, *got), *in_hbm(*hs), *in_hbm(*prior))


def wide_sum(*parts):
    parts = [jnp.concatenate(p, axis=1) if isinstance(p, list) else p for p in parts]
    return functools.reduce(lambda a, b: a + b, [p.astype(F32) for p in parts])


def add_kernel(*refs):
    q, others, out = refs[0], refs[1:-1], refs[-1]
    pieces, wide = others[-PIECES:], others[:-PIECES]
    run = pieces[0].shape[1]
    for k, piece in enumerate(pieces):
        part = pl.ds(k * run, run)
        total = q[:, part].astype(F32) + piece[...].astype(F32)
        for ref in wide:
            total += ref[:, part].astype(F32)
        out[:, part] = total.astype(out.dtype)


def add_parts(q, pieces, *more):
    return pl.pallas_call(
        add_kernel,
        in_specs=[VMEM] * (1 + len(more) + len(pieces)),
        out_specs=VMEM,
        out_shape=jax.ShapeDtypeStruct(q.shape, BF16),
        compiler_params=params(12),
        cost_estimate=cost(0, 0),
        name="add_parts",
    )(q, *more, *pieces)


def pair_kernel(a, b, out):
    out[...] = (a[...].astype(F32) + b[...].astype(F32)).astype(out.dtype)


def add_pair(a, b):
    return pl.pallas_call(
        pair_kernel,
        in_specs=[VMEM] * 2,
        out_specs=VMEM,
        out_shape=jax.ShapeDtypeStruct(a.shape, BF16),
        compiler_params=params(8),
        cost_estimate=cost(0, 0),
        name="add_pair",
    )(a, b)


def base_kernel(grad, bias, q, *refs):
    pieces, wide, out = refs[:PIECES], refs[PIECES:-1], refs[-1]
    run = pieces[0].shape[1]
    for k, piece in enumerate(pieces):
        part = pl.ds(k * run, run)
        total = q[:, part].astype(F32) + piece[...].astype(F32)
        for ref in wide:
            total += ref[:, part].astype(F32)
        total += bias[:, part].astype(F32)
        out[:, part] = (grad[:, part].astype(F32) * total).astype(out.dtype)


def base_grads(grad, bias, q, pieces, *more):
    return pl.pallas_call(
        base_kernel,
        in_specs=[VMEM] * (3 + len(pieces) + len(more)),
        out_specs=VMEM,
        out_shape=jax.ShapeDtypeStruct(grad.shape, BF16),
        compiler_params=params(16),
        cost_estimate=pl.CostEstimate(flops=1, bytes_accessed=grad.size, transcendentals=0),
        name="base_grads",
    )(grad, bias[None, :], q, *pieces, *more)


def line_pairs(hops):
    return [(2 * a + core, 2 * b + core) for a, b in hops for core in (0, 1)]


def after(value, *done):
    return lax.optimization_barrier((value,) + done)[0]


def on_line(base_input, layer_input, out_grad, cross_weight, cross_bias):
    lanes = base_input.shape[0]
    col, row = lax.axis_index("col"), lax.axis_index("row")
    z, core = col // 2, col % 2
    end = jnp.logical_or(z == 0, z == 3)
    first = jnp.where(z < 2, 3, 0)
    place = jnp.stack([core, z, row, first, row ^ first]).astype(jnp.int32)

    def across(a, name):
        with jax.named_scope(name):
            return jax.tree.map(lambda one: lax.ppermute(one, "col", [(i, i ^ 1) for i in range(8)]), a)

    def line(a, hops, name):
        with jax.named_scope(name):
            return lax.ppermute(a, "col", line_pairs(hops))

    def plane(a, hops, name):
        pairs = [(8 * f + 2 * k + c, 8 * t + 2 * k + c) for k in range(4) for c, f, t in hops(k)]
        with jax.named_scope(name):
            return lax.ppermute(a, ("row", "col"), pairs)

    def first_way(k):
        return [(c, r, r ^ (1 + c)) for c in (0, 1) for r in range(4)]

    def second_way(k):
        return [(c, r, r ^ (2 - c)) for c in (0, 1) for r in range(4)]

    outer, inner = [(0, 1), (1, 0), (2, 3), (3, 2)], [(1, 2), (2, 1)]
    outwards, inwards = [(1, 0), (2, 3)], [(0, 1), (3, 2)]

    cross_weight = pltpu.with_memory_space_constraint(cross_weight, pltpu.VMEM)
    def pre(turns, slots, got, *done, prior=()):
        return list(pre_parts(after(place, *done), layer_input, got, cross_weight, turns, slots, 8, prior))

    def back(slots, hs, *done, prior=None, by_role=True):
        return back_parts(after(place, *done), slots, hs, cross_weight, 8, prior, by_role)

    def both(*values, done):
        return lax.optimization_barrier(values + tuple(done))[: len(values)]

    relays = turned(place, place[REL]) == 1
    p1 = plane(layer_input, first_way, "p1")
    own_h = (out_grad.astype(F32) * base_input.astype(F32)).astype(BF16)
    a0, b0 = line(own_h, outer, "a0"), line(own_h, inner, "b0")
    h0 = across(own_h, "h0")
    each = 1 + PIECES
    q = pre((0,), (0, 1, 2, 3), (), own_h)
    p1 = after(p1, q[0])
    to_p2 = jnp.where(relays, p1, layer_input)
    to_p3 = jnp.where(relays, layer_input, p1)
    p2 = plane(to_p2, second_way, "p2")
    roles = back((0,), (own_h, h0), to_p2, to_p3)

    a0, b0, p2, to_p3 = both(a0, b0, p2, to_p3, done=roles)
    a1, b1 = line(b0, outwards, "a1"), line(a0, inner, "b1")
    p3 = plane(to_p3, second_way, "p3")
    h1 = across(a0, "h1")
    q[: 2 * each] = pre((1,), (0, 1), (p1, p2), prior=q[: 2 * each])
    q0, o0 = q[0], across(q[1:each], "o0")
    to_ra1 = add_parts(after(q0, p3), o0)
    ra1 = line(to_ra1, inwards, "ra1")
    q[each:] = pre((2, 3), (1, 2, 3), (p1, p2, p3), to_ra1, prior=q[each:])
    q1, q2, q3 = q[each], q[2 * each], q[3 * each]
    o1, o2, o3 = [across(q[k * each + 1 : (k + 1) * each], f"o{k}") for k in (1, 2, 3)]

    a1, b1 = both(a1, b1, done=(q1,))
    a2 = line(b1, outwards, "a2")
    s2 = jnp.where(end, a1, b0)
    h2 = across(s2, "h2")

    ra1, q0 = both(ra1, q0, done=(s2,))
    to_rb2, to_ra2 = add_parts(q0, o0, ra1), add_parts(q1, o1)
    rb2, ra2 = line(to_rb2, inner, "rb2"), line(to_ra2, inwards, "ra2")
    roles = back((1, 2), (a0, h1, s2, h2), to_rb2, to_ra2, *o2, prior=roles)

    a2, *roles = both(a2, *roles, done=())
    s3 = jnp.where(end, a2, b1)
    h3 = across(s3, "h3")
    rb2, ra2 = both(rb2, ra2, done=(s3,))
    mine, near, relayed, far = back((3,), (s3, h3), rb2, ra2, prior=roles)

    rb2, ra2 = both(rb2, ra2, done=(far,))
    to_ra3, to_rb3 = add_parts(q2, o2, rb2), add_parts(q1, o1, ra2)
    ra3, rb3 = line(to_ra3, outer, "ra3"), line(to_rb3, inner, "rb3")

    f1, e1 = plane(far, first_way, "f1"), plane(near, first_way, "e1")
    hs = (own_h, h0, a0, h1, s2, h2, s3, h3)
    tile = 512
    tiles = base_input.shape[1] // tile
    early = tiles * 5 // 8
    got = (p1, p2, p3)
    grads = weight_grads(after(place, to_ra3, to_rb3), layer_input, got, hs, tile, 0, early)
    to_e2 = add_pair(relayed, after(f1, *grads))
    e2 = plane(to_e2, second_way, "e2")
    grad, bias = weight_grads(after(place, to_e2), layer_input, got, hs, tile, early, tiles - early, grads)
    ra3, rb3, e1, *o3 = both(ra3, rb3, e1, *o3, done=(bias,))
    base_grad = base_grads(out_grad, cross_bias, q3, o3, ra3, rb3)
    branch = wide_sum(mine, e1, after(e2, base_grad)).astype(BF16)
    return (grad, bias[0], base_grad, branch)


def on_any(base_input, layer_input, out_grad, cross_weight, cross_bias):
    input_panel = lax.all_gather(layer_input, "row", axis=0, tiled=True)
    hidden = (out_grad.astype(F32) * base_input.astype(F32)).astype(BF16)
    hidden_panel = lax.all_gather(hidden, "col", axis=0, tiled=True)
    weight_grad = lax.dot_general(
        hidden_panel, input_panel, (((0,), (0,)), ((), ())), preferred_element_type=F32
    )
    bias_grad = jnp.sum(hidden_panel, axis=0, dtype=F32)
    part = lax.dot_general(input_panel, cross_weight, (((1,), (1,)), ((), ())), preferred_element_type=F32)
    preact = lax.psum_scatter(part.astype(BF16), "col", scatter_dimension=0, tiled=True).astype(F32)
    preact = preact + cross_bias.astype(F32)[None, :]
    base_grad = (out_grad.astype(F32) * preact).astype(BF16)
    part = jnp.dot(hidden_panel, cross_weight, preferred_element_type=F32).astype(BF16)
    branch = lax.psum_scatter(part, "row", scatter_dimension=0, tiled=True)
    return (weight_grad, bias_grad, base_grad, branch)


def solution(mesh):
    in_specs = (P("col", "row"), P("row", "col"), P("col", "row"), P("row", "col"), P("row"))
    out_specs = (P("row", "col"), P("row"), P("col", "row"), P("row", "col"))
    body = on_line if (mesh.shape["row"], mesh.shape["col"]) == (4, 8) else on_any
    return jax.shard_map(body, mesh=mesh, in_specs=in_specs, out_specs=out_specs, check_vma=False)
```
